256 devices in a mesh: layer: 2 (over core), seq: 32 (over z, x), head: 4 (over y).
Axes of the slice: x: 4, y: 4, z: 8, core: 2. Of those that a mesh axis runs over, the one named last changes fastest.
Arguments:
- seed_grad: bfloat16 [8192, 4608], P('seq', 'head'), may hold values from -6 to 6
- queries: bfloat16 [2, 8192, 2048], P('layer', 'seq', 'head'), may hold values from -12 to 12
- key_cache: bfloat16 [2, 8192, 1024], P('layer', 'seq', 'head'), may hold values from -6 to 6
- w_out: bfloat16 [2, 2048, 4608], P('layer', 'head'), may hold values from -0.09375 to 0.09375
- w_value: bfloat16 [2, 4608, 1024], P('layer', None, 'head'), may hold values from -0.09375 to 0.09375
- norm_gain: float32 [2, 4608], P('layer'), may hold values from 0.5 to 2
- inv_rms: float32 [2, 8192], P('layer', 'seq'), may hold values from 0.3 to 3
- decoder_pool: bfloat16 [2, 8, 128, 4608], P('layer', None, None, 'head'), may hold values from -0.09375 to 0.09375
- active: int32 [2, 64, 8], P('layer', 'seq'), may hold values from -1 to 7
- feature_acts: bfloat16 [2, 64, 8, 128, 128], P('layer', 'seq', 'head'), may hold values from 0.049804688 to 3
Outputs:
- edges: bfloat16 [2, 64, 8, 128, 128], P('layer', 'seq', 'head')
- resid_grad: bfloat16 [2, 8192, 4608], P('layer', 'seq', 'head')
The draws below stay inside these ranges and needn't reach their ends.
Inputs may be any that keep to these rules, and one draw needn't show every extreme that they name: `active`: each entry is -1 (padding) or a pool slot of that layer.
All inputs are finite; a program needn't handle non-finite values.
Results may differ from the reference program's by a relative error of at most 0.013.
Values may be sent and summed in bfloat16 or wider, within the bound.
No kernel may reach another device: no remote copies, remote signals or barrier semaphores. Data moves between devices by JAX's collectives and lax.ppermute only.
A program may use at most 64 MiB of HBM per device.

```python
import math
import jax
import jax.numpy as jnp
from jax import lax

D = 4608
HD = 128
QH = 16
KVH = 8
TILE = 128
WINDOW = 4096
POOL = 8
LAYERS = 2
TOKENS = 8192
TILES = 64
OWN = 8


def touch_ends(values, own_key, low, largest):
    dims = values.shape
    spot = [jax.random.randint(jax.random.fold_in(own_key, axis), (), 0, dims[axis]) for axis in range(len(dims))]
    values = values.at[tuple(spot)].set(low)
    longest = dims.index(max(dims))
    spot[longest] = (spot[longest] + 1) % dims[longest]
    return values.at[tuple(spot)].set(largest)


def shard_levels(stream_key, shape, pieces, low, top_value):
    def one(axis_at, shards_of):
        draws = jax.random.uniform(jax.random.fold_in(jax.random.fold_in(stream_key, 6), axis_at), (shards_of,), jnp.float32, low / len(pieces), top_value / len(pieces))
        return jnp.repeat(jnp.exp(draws), shape[axis_at] // shards_of).reshape((-1,) + (1,) * (len(shape) - axis_at - 1))

    gain = one(*pieces[0])
    for cut in pieces[1:]:
        gain = gain * one(*cut)
    return gain


def centred(stream_key, dims, scale, limit, cuts=(), held_as=jnp.bfloat16):
    array = jax.random.normal(stream_key, dims, jnp.float32) * scale
    if len(cuts) > 0:
        array = shard_levels(stream_key, dims, cuts, -0.22, 0.18) * array
    return jnp.clip(array, min=-limit, max=limit).astype(held_as)


def setup_inputs(seed: int = 0) -> dict:
    key_of = jax.random.split(jax.random.key(seed), 11)
    return {
        "seed_grad": centred(key_of[0], (TOKENS, D), 1.0, 6.0, ((0, 32), (1, 4))),
        "queries": centred(key_of[1], (LAYERS, TOKENS, QH * HD), 2.0, 12.0, ((0, 2), (1, 32), (2, 4))),
        "key_cache": centred(key_of[2], (LAYERS, TOKENS, KVH * HD), 1.0, 6.0, ((0, 2), (1, 32), (2, 4))),
        "w_out": centred(key_of[3], (LAYERS, QH * HD, D), D ** -0.5, 0.09375, ((0, 2), (1, 4))),
        "w_value": centred(key_of[4], (LAYERS, D, KVH * HD), D ** -0.5, 0.09375, ((0, 2), (2, 4))),
        "norm_gain": jnp.clip(jnp.exp(math.log(2.0) - 1.3862944 * jax.random.uniform(key_of[5], (LAYERS, D), jnp.float32) ** shard_levels(key_of[5], (LAYERS, D), ((0, 2),), -0.2, 0.2)), 0.5, 2.0),
        "inv_rms": jnp.clip(jnp.exp(math.log(3.0) - 2.3025851 * jax.random.uniform(key_of[6], (LAYERS, TOKENS), jnp.float32) ** shard_levels(key_of[6], (LAYERS, TOKENS), ((0, 2), (1, 32)), -0.2, 0.2)), 0.3, 3.0),
        "decoder_pool": centred(key_of[7], (LAYERS, POOL, TILE, D), D ** -0.5, 0.09375, ((0, 2), (3, 4))),
        "active": touch_ends(jax.random.randint(key_of[8], (LAYERS, TILES, OWN), -1, POOL), jax.random.fold_in(key_of[8], 1), -1, POOL - 1).astype(jnp.int32),
        "feature_acts": jnp.clip(jnp.exp(math.log(3.0) - 4.0982585 * jax.random.uniform(key_of[9], (LAYERS, TILES, OWN, TILE, TILE), jnp.float32) ** shard_levels(key_of[9], (LAYERS, TILES, OWN, TILE, TILE), ((0, 2), (1, 32), (2, 4)), -0.2, 0.2)), 0.049804688, 3.0).astype(jnp.bfloat16),
    }


softcap = 50.0
query_scale = 1.0 / 12.0


def reference(seed_grad, queries, key_cache, w_out, w_value, norm_gain, inv_rms, decoder_pool, active, feature_acts):
    group = QH // KVH
    positions = jnp.arange(TOKENS, dtype=jnp.int32)
    causal_keep = positions[None, :] <= positions[:, None]
    window_keep = causal_keep & ((positions[:, None] - positions[None, :]) < WINDOW)
    contribs = []
    for layer_index in range(LAYERS):
        layer_keep = window_keep if layer_index % 2 == 0 else causal_keep
        d_out = lax.dot_general(seed_grad, w_out[layer_index], (((1,), (1,)), ((), ())), preferred_element_type=jnp.float32).astype(jnp.bfloat16)
        query_four = queries[layer_index].reshape(TOKENS, KVH, group, HD).transpose(1, 0, 2, 3)
        key_three = key_cache[layer_index].reshape(TOKENS, KVH, HD).transpose(1, 0, 2)
        grad_four = d_out.reshape(TOKENS, KVH, group, HD).transpose(1, 0, 2, 3)

        def per_kv(items, layer_keep=layer_keep):
            query_rows, key_rows, grad_rows = items
            raw_scores = jnp.einsum('pgd,qd->gpq', query_rows.astype(jnp.float32), key_rows.astype(jnp.float32))
            capped = softcap * jnp.tanh(raw_scores * query_scale / softcap)
            expo = jnp.where(layer_keep[None], jnp.exp(capped), 0.0)
            totals = jnp.sum(expo, axis=-1)
            weights = (expo / totals[..., None]).astype(jnp.bfloat16)
            return jnp.einsum('gpq,pgd->qd', weights.astype(jnp.float32), grad_rows.astype(jnp.float32))

        value_grads = lax.map(per_kv, (query_four, key_three, grad_four))
        value_grads = value_grads.transpose(1, 0, 2).reshape(TOKENS, KVH * HD).astype(jnp.bfloat16)
        product = lax.dot_general(value_grads, w_value[layer_index], (((1,), (1,)), ((), ())), preferred_element_type=jnp.float32)
        contribs.append(product * norm_gain[layer_index][None, :] * inv_rms[layer_index][:, None])
    resid_list = []
    edge_list = []
    upper_sum = jnp.zeros((TOKENS, D), jnp.float32)
    uppers = [None] * LAYERS
    for layer_index in range(LAYERS - 1, -1, -1):
        upper_sum = upper_sum + contribs[layer_index]
        uppers[layer_index] = upper_sum
    for layer_index in range(LAYERS):
        resid = (seed_grad.astype(jnp.float32) + uppers[layer_index]).astype(jnp.bfloat16)
        resid_list.append(resid)
        token_tiles = resid.reshape(TILES, TILE, D).astype(jnp.float32)
        partial_dots = jnp.einsum('tid,pjd->tpij', token_tiles, decoder_pool[layer_index].astype(jnp.float32), precision=lax.Precision.HIGHEST)
        slot_index = active[layer_index]
        slot_safe = jnp.maximum(slot_index, 0)
        chosen = jnp.take_along_axis(partial_dots, slot_safe[:, :, None, None], axis=1)
        chosen = jnp.where(slot_index[:, :, None, None] >= 0, chosen, 0.0)
        edge_list.append((chosen * feature_acts[layer_index].astype(jnp.float32)).astype(jnp.bfloat16))
    return jnp.stack(edge_list), jnp.stack(resid_list)
```

```python
import functools
import math

import jax
import jax.numpy as jnp
from jax import lax
from jax.experimental import pallas as pl
from jax.experimental.pallas import tpu as pltpu
from jax.sharding import Mesh, PartitionSpec as P

HD = 128
TILE = 128
WINDOW = 4096
SOFTCAP = 50.0
TO_TANH = 1.0 / 12.0 / SOFTCAP
TO_EXP2 = SOFTCAP * math.log2(math.e)

NX = 4
NP = 4
BLK = 256
VMEM_CAP = 56 * 1024 * 1024


def rotate(a, axis, d):
    n = lax.axis_size(axis)
    return lax.ppermute(a, axis, [(i, (i + d) % n) for i in range(n)])


def to_chip(a, flip, d):
    pairs = [(z * NX + x, (z ^ flip) * NX + (x + d) % NX) for z in range(2 * NP) for x in range(NX)]
    return lax.ppermute(a, ("z", "x"), pairs)


def after(a, *others):
    return lax.optimization_barrier((a,) + others)[0]


def nt_dot(a, b):
    return lax.dot_general(a, b, (((1,), (1,)), ((), ())), preferred_element_type=jnp.float32)


VM = pl.BlockSpec(memory_space=pltpu.VMEM)
SM = pl.BlockSpec(memory_space=pltpu.SMEM)


def params():
    return pltpu.CompilerParams(vmem_limit_bytes=VMEM_CAP)


def dout_kernel(place, w, *refs):
    own, other, (mine, partner) = refs[0:4], refs[4:8], refs[8:10]
    layer, y, z0 = place[3], place[4], place[1]
    cols = own[0].shape[1]
    for out, half in ((partner, 1 - z0), (mine, z0)):
        rows = pl.ds(pl.multiple_of(half * 2 * HD, 2 * HD), 2 * HD)
        for pieces, at in ((own, layer), (other, 1 - layer)):
            total = jnp.zeros((2 * HD, BLK // 2), jnp.float32)
            for d in range(4):
                first = pl.multiple_of(lax.rem(y - d + 4, 4) * cols, 128)
                total += nt_dot(w[rows, pl.ds(first, cols)], pieces[d][...])
            out[:, pl.ds(pl.multiple_of(at * (BLK // 2), 128), BLK // 2)] = total.astype(jnp.bfloat16)


def dout(place, w, own, other):
    shape = jax.ShapeDtypeStruct((2 * HD, BLK), jnp.bfloat16)
    return pl.pallas_call(
        dout_kernel,
        out_shape=(shape, shape),
        in_specs=[SM] + [VM] * 9,
        out_specs=(VM, VM),
        compiler_params=params(),
        name="dout",
    )(place, w, *own, *other)


def expo_kernel(place, *refs):
    queries, keys = refs[0:4], refs[4:8]
    expo, sums, q_all, k_all, acc = refs[8:]
    z1, z0, x, layer = place[0], place[1], place[2], place[3]
    step = pl.program_id(0)

    @pl.when(step == 0)
    def _():
        for d in range(4):
            q_all[d] = queries[d][...]
            k_all[d] = keys[d][...]
        acc[...] = jnp.zeros_like(acc)

    e, key_r = step // 2, step % 2
    key_z = 2 * (z1 - e) + (z0 ^ key_r)

    def one(qb, carry):
        d, r = qb // 2, qb % 2
        query_z = 2 * z1 + (z0 ^ r)
        apart = (query_z - key_z) * NX + lax.rem(x - d + NX, NX) - x
        keep = (e <= z1) & (apart >= 0) & ((layer == 1) | (apart <= WINDOW // BLK))
        edge = (apart == 0) | ((layer == 0) & (apart == WINDOW // BLK))

        def work(masked):
            for g in range(2):
                s = nt_dot(k_all[e, key_r], q_all[d, r, :, g * HD : (g + 1) * HD])
                ex = jnp.exp2(jnp.tanh(s * TO_TANH) * TO_EXP2)
                if masked:
                    key_at = lax.broadcasted_iota(jnp.int32, (BLK, BLK), 0)
                    query_at = lax.broadcasted_iota(jnp.int32, (BLK, BLK), 1)
                    low = jnp.where(apart == 0, 0, 1)
                    inside = jnp.where(low == 0, query_at - key_at, key_at - query_at - 1) >= 0
                    ex = jnp.where(inside, ex, 0.0)
                acc[g, d, r] += jnp.sum(ex.reshape(BLK // 8, 8, BLK), axis=0)
                at = pl.multiple_of((g * 8 + qb) * BLK, BLK)
                expo[0, :, pl.ds(at, BLK)] = ex.astype(jnp.bfloat16)

        @pl.when(keep & jnp.logical_not(edge))
        def _():
            work(False)

        @pl.when(keep & edge)
        def _():
            work(True)

        @pl.when(jnp.logical_not(keep))
        def _():
            for g in range(2):
                at = pl.multiple_of((g * 8 + qb) * BLK, BLK)
                expo[0, :, pl.ds(at, BLK)] = jnp.zeros((BLK, BLK), jnp.bfloat16)

        return carry

    lax.fori_loop(0, 8, one, 0)

    @pl.when(step == 7)
    def _():
        for d in range(4):
            for r in range(2):
                for g in range(2):
                    row = r * 2 + g
                    sums[lax.rem(x - d + NX, NX), row : row + 1, :] = jnp.sum(acc[g, d, r], axis=0, keepdims=True)


def expo_call(place, queries, keys):
    whole = [pl.BlockSpec((2, BLK, 2 * HD), lambda i: (0, 0, 0))] * 4 + [pl.BlockSpec((2, BLK, HD), lambda i: (0, 0, 0))] * 4
    return pl.pallas_call(
        expo_kernel,
        grid=(8,),
        out_shape=(
            jax.ShapeDtypeStruct((8, BLK, 16 * BLK), jnp.bfloat16),
            jax.ShapeDtypeStruct((NX, 4, BLK), jnp.float32),
        ),
        in_specs=[SM] + whole,
        out_specs=(
            pl.BlockSpec((1, BLK, 16 * BLK), lambda i: (i, 0, 0)),
            pl.BlockSpec((NX, 4, BLK), lambda i: (0, 0, 0)),
        ),
        scratch_shapes=[
            pltpu.VMEM((4, 2, BLK, 2 * HD), jnp.bfloat16),
            pltpu.VMEM((4, 2, BLK, HD), jnp.bfloat16),
            pltpu.VMEM((2, 4, 2, 8, BLK), jnp.float32),
        ],
        compiler_params=params(),
        name="expo",
    )(place, *queries, *keys)


def grads_kernel(place, expo, *refs):
    grads, sums = refs[0:8], refs[8:12]
    out_own, out_far, scaled = refs[12:]
    x = place[2]
    step = pl.program_id(0)

    @pl.when(step == 0)
    def _():
        for d in range(4):
            at = lax.rem(x - d + NX, NX)
            total = sums[0][at] + sums[1][at] + sums[2][at] + sums[3][at]
            inverse = 1.0 / total
            for r in range(2):
                for g in range(2):
                    piece = grads[d * 2 + r][g * HD : (g + 1) * HD, :].astype(jnp.float32)
                    row = r * 2 + g
                    first = (g * 8 + d * 2 + r) * BLK
                    scaled[:, first : first + BLK] = (piece * inverse[row : row + 1, :]).astype(jnp.bfloat16)

    part = nt_dot(expo[0], scaled[...])

    @pl.when(step < 2)
    def _():
        out_own[step % 2] = part

    @pl.when(step >= 2)
    def _():
        out_far[step // 2 - 1, step % 2] = part.astype(jnp.bfloat16)


def grads_call(place, expo, grads, sums):
    return pl.pallas_call(
        grads_kernel,
        grid=(8,),
        out_shape=(
            jax.ShapeDtypeStruct((2, BLK, HD), jnp.float32),
            jax.ShapeDtypeStruct((3, 2, BLK, HD), jnp.bfloat16),
        ),
        in_specs=[SM, pl.BlockSpec((1, BLK, 16 * BLK), lambda i: (i, 0, 0))]
        + [pl.BlockSpec((2 * HD, BLK), lambda i: (0, 0))] * 8
        + [pl.BlockSpec((NX, 4, BLK), lambda i: (0, 0, 0))] * 4,
        out_specs=(
            pl.BlockSpec((2, BLK, HD), lambda i: (0, 0, 0)),
            pl.BlockSpec((3, 2, BLK, HD), lambda i: (0, 0, 0, 0)),
        ),
        scratch_shapes=[pltpu.VMEM((HD, 16 * BLK), jnp.bfloat16)],
        compiler_params=params(),
        name="value_grads",
    )(place, expo, *grads, *sums)


def contrib_kernel(v0, v1, v2, v3, w0, w1, w2, w3, gain, inv, out):
    total = nt_dot(v0[...], w0[...])
    for v, w in ((v1, w1), (v2, w2), (v3, w3)):
        total += nt_dot(v[...], w[...])
    out[...] = total * gain[...] * inv[...]


def contrib_call(values, weights, gain, inv):
    cols = weights[0].shape[0]
    return pl.pallas_call(
        contrib_kernel,
        out_shape=jax.ShapeDtypeStruct((BLK, cols), jnp.float32),
        in_specs=[VM] * 10,
        out_specs=VM,
        compiler_params=params(),
        name="contrib",
    )(*values, *weights, gain, inv)


def edges_kernel(place, active, seed, contrib, higher, pool, resid, own, *far):
    y = place[4]
    resid[...] = (seed[...].astype(jnp.float32) + (higher[...] + contrib[...])).astype(jnp.bfloat16)
    for d in range(4):
        owner = lax.rem(y + d, 4)
        for t in range(2):
            rows = resid[t * TILE : (t + 1) * TILE, :]
            for k in range(2):
                slot = active[t, owner * 2 + k]
                dots = nt_dot(rows, pool[jnp.maximum(slot, 0)])
                dots = jnp.where(slot >= 0, dots, 0.0)
                if d == 0:
                    own[t, k] = dots
                else:
                    far[d - 1][t, k] = dots.astype(jnp.bfloat16)


def edges_call(place, active, seed, contrib, higher, pool):
    far = jax.ShapeDtypeStruct((2, 2, TILE, TILE), jnp.bfloat16)
    return pl.pallas_call(
        edges_kernel,
        out_shape=(
            jax.ShapeDtypeStruct(seed.shape, jnp.bfloat16),
            jax.ShapeDtypeStruct((2, 2, TILE, TILE), jnp.float32),
            far,
            far,
            far,
        ),
        in_specs=[SM, SM] + [VM] * 4,
        out_specs=(VM,) * 5,
        compiler_params=params(),
        name="edges",
    )(place, active, seed, contrib, higher, pool)


def local(
    seed_grad,
    queries,
    key_cache,
    w_out,
    w_value,
    norm_gain,
    inv_rms,
    decoder_pool,
    active,
    feature_acts,
):
    z, x, y, layer = (lax.axis_index(a) for a in ("z", "x", "head", "layer"))
    z1, z0 = z // 2, z % 2
    place = jnp.stack([z1, z0, x, layer, y]).astype(jnp.int32)
    cols = seed_grad.shape[1]
    flip = [(i, i ^ 1) for i in range(2 * NP)]

    q, k = queries[0], key_cache[0]

    def heads_of(half):
        return (
            lax.dynamic_slice_in_dim(q, half * 2 * HD, 2 * HD, 1),
            lax.dynamic_slice_in_dim(k, half * HD, HD, 1),
        )

    q_mine, k_mine = heads_of(z0)
    q_theirs, k_theirs = heads_of(1 - z0)
    q_from = lax.ppermute(q_theirs, "z", flip)
    k_from = lax.ppermute(k_theirs, "z", flip)

    half = lax.dynamic_slice_in_dim(seed_grad, layer * (BLK // 2), BLK // 2, 0)
    own = [half] + [rotate(half, "head", d) for d in (1, 2, 3)]
    other = [rotate(a, "layer", 1) for a in own]

    q_pair = jnp.stack([q_mine, q_from])
    k_pair = jnp.stack([k_mine, k_from])
    q_all = [q_pair] + [rotate(q_pair, "x", d) for d in (1, 2, 3)]
    k_all = [k_pair] + [rotate(k_pair, "z", 2 * e) for e in (1, 2, 3)]

    d_mine, d_theirs = dout(place, w_out[0], own, other)
    grads = []
    for d in range(4):
        grads.append(d_mine if d == 0 else to_chip(d_mine, 0, d))
        grads.append(to_chip(d_theirs, 1, d))

    expo, sums = expo_call(place, q_all, k_all)
    sums = [sums] + [rotate(sums, "x", d) for d in (1, 2, 3)]
    wv = after(w_value[0], own[1], own[2], own[3])
    w_cols = []
    for d in range(4):
        block = lax.dynamic_slice_in_dim(wv, lax.rem(y + d, 4) * cols, cols, 0)
        w_cols.append(block if d == 0 else rotate(block, "head", d))

    near, far = grads_call(place, expo, grads, sums)
    total = near
    for e in (1, 2, 3):
        total = total + rotate(far[e - 1], "z", -2 * e).astype(jnp.float32)
    total = total.astype(jnp.bfloat16)
    v_from = lax.ppermute(total[1], "z", flip)
    values = jnp.where(
        z0 == 0,
        jnp.concatenate([total[0], v_from], axis=1),
        jnp.concatenate([v_from, total[0]], axis=1),
    )
    values = [values] + [rotate(values, "head", d) for d in (1, 2, 3)]
    gain = lax.dynamic_slice_in_dim(norm_gain, y * cols, cols, 1)
    contrib = contrib_call(values, w_cols, gain, inv_rms.reshape(BLK, 1))
    higher = lax.ppermute(contrib, "layer", [(1, 0)])
    resid, mine, *parts = edges_call(place, active[0], seed_grad, contrib, higher, decoder_pool[0])
    for d in (1, 2, 3):
        mine = mine + rotate(parts[d - 1], "head", d).astype(jnp.float32)
    edges = (mine * feature_acts[0].astype(jnp.float32)).astype(jnp.bfloat16)
    return edges[None], resid[None]


def solution(mesh):
    fine = Mesh(mesh.devices.reshape(2, 2 * NP, NX, 4), ("layer", "z", "x", "head"))
    seq = ("z", "x")
    placed = (
        P(seq, "head"),
        P("layer", seq, "head"),
        P("layer", seq, "head"),
        P("layer", "head", None),
        P("layer", None, "head"),
        P("layer", None),
        P("layer", seq),
        P("layer", None, None, "head"),
        P("layer", seq, None),
        P("layer", seq, "head", None, None),
    )
    return jax.shard_map(
        local,
        mesh=fine,
        in_specs=placed,
        out_specs=(P("layer", seq, "head", None, None), P("layer", seq, "head")),
        check_vma=False,
    )
```

```python
import functools
import math

import jax
import jax.numpy as jnp
from jax import lax
from jax.experimental import pallas as pl
from jax.experimental.pallas import tpu as pltpu
from jax.sharding import Mesh, PartitionSpec as P

HD = 128
TILE = 128
WINDOW = 4096
SOFTCAP = 50.0
TO_TANH = 1.0 / 12.0 / SOFTCAP
TO_EXP2 = SOFTCAP * math.log2(math.e)

NX = 4
NP = 4
BLK = 256


def rotate(a, axis, d):
    n = lax.axis_size(axis)
    return lax.ppermute(a, axis, [(i, (i + d) % n) for i in range(n)])


def along_pairs(a, e, back):
    pairs = []
    for layer in range(2):
        for z1 in range(NP - e):
            near, far = layer * NP + z1, layer * NP + z1 + e
            if layer == 1 or e * 2 - 1 <= WINDOW // (BLK * NX):
                pairs.append((far, near) if back else (near, far))
    return lax.ppermute(a, ("layer", "z1"), pairs)


def after(a, *others):
    return lax.optimization_barrier((a,) + others)[0]


def nt_dot(a, b):
    return lax.dot_general(a, b, (((1,), (1,)), ((), ())), preferred_element_type=jnp.float32)


VM = pl.BlockSpec(memory_space=pltpu.VMEM)
SM = pl.BlockSpec(memory_space=pltpu.SMEM)
HB = pl.BlockSpec(memory_space=pltpu.HBM)


def in_hbm(a):
    return pltpu.with_memory_space_constraint(a, pltpu.HBM)


def params(mib, us):
    return dict(
        compiler_params=pltpu.CompilerParams(vmem_limit_bytes=mib * 1024 * 1024),
        cost_estimate=pl.CostEstimate(flops=int(us * 1e9), bytes_accessed=0, transcendentals=0),
    )


def parts_kernel(place, seed, q, k, gain, half, q_mine, k_mine, qk_theirs, gain_cols, sems):
    z0, layer, y = place[1], place[3], place[4]
    cols = half.shape[1]
    moves = (
        (seed.at[pl.ds(pl.multiple_of(layer * (BLK // 2), BLK // 2), BLK // 2), :], half),
        (q.at[:, pl.ds(pl.multiple_of((1 - z0) * 2 * HD, 2 * HD), 2 * HD)], qk_theirs.at[:, : 2 * HD]),
        (k.at[:, pl.ds(pl.multiple_of((1 - z0) * HD, HD), HD)], qk_theirs.at[:, 2 * HD :]),
        (q.at[:, pl.ds(pl.multiple_of(z0 * 2 * HD, 2 * HD), 2 * HD)], q_mine),
        (k.at[:, pl.ds(pl.multiple_of(z0 * HD, HD), HD)], k_mine),
        (gain.at[:, pl.ds(pl.multiple_of(y * cols, 128), cols)], gain_cols),
    )
    copies = [pltpu.make_async_copy(a, b, sems.at[i]) for i, (a, b) in enumerate(moves)]
    for copy in copies:
        copy.start()
    for copy in copies:
        copy.wait()


def parts_call(place, seed, q, k, gain):
    cols = seed.shape[1]
    b16 = jnp.bfloat16
    return pl.pallas_call(
        parts_kernel,
        out_shape=(
            jax.ShapeDtypeStruct((BLK // 2, cols), b16),
            jax.ShapeDtypeStruct((BLK, 2 * HD), b16),
            jax.ShapeDtypeStruct((BLK, HD), b16),
            jax.ShapeDtypeStruct((BLK, 3 * HD), b16),
            jax.ShapeDtypeStruct((1, cols), jnp.float32),
        ),
        in_specs=[SM] + [HB] * 4,
        out_specs=(VM,) * 5,
        scratch_shapes=[pltpu.SemaphoreType.DMA((6,))],
        name="parts",
        **params(8, 1),
    )(place, in_hbm(seed), in_hbm(q), in_hbm(k), in_hbm(gain))


def rows_kernel(place, w, *refs):
    outs, sems = refs[:4], refs[4]
    y = place[4]
    cols = outs[0].shape[0]
    copies = []
    for d, out in enumerate(outs):
        rows = pl.ds(pl.multiple_of(lax.rem(y + d, 4) * cols, 128), cols)
        copies.append(pltpu.make_async_copy(w.at[rows, :], out, sems.at[d]))
        copies[d].start()
    for copy in copies:
        copy.wait()


def rows_call(place, w):
    shape = jax.ShapeDtypeStruct((w.shape[0] // 4, w.shape[1]), w.dtype)
    return pl.pallas_call(
        rows_kernel,
        out_shape=(shape,) * 4,
        in_specs=[SM, HB],
        out_specs=(VM,) * 4,
        scratch_shapes=[pltpu.SemaphoreType.DMA((4,))],
        name="rows",
        **params(12, 1),
    )(place, in_hbm(w))


def total_kernel(place, near, far0, far1, far2, out):
    for r in range(2):
        total = near[r]
        for far in (far0, far1, far2):
            total += far[r].astype(jnp.float32)
        total = total.astype(out.dtype)
        for y in range(4):
            out[(place[1] ^ r) * 4 + y] = total


def total_call(place, near, far):
    return pl.pallas_call(
        total_kernel,
        out_shape=jax.ShapeDtypeStruct((8, BLK, HD), jnp.bfloat16),
        in_specs=[SM] + [VM] * 4,
        out_specs=VM,
        name="total",
        **params(8, 1),
    )(place, near, *far)


def dout_kernel(place, w, own, other, mine, theirs, w_all, sems):
    z0, layer, y = place[1], place[3], place[4]
    cols = own.shape[2]
    part = BLK // 2
    copies = []
    for d in range(4):
        first = pl.multiple_of(lax.rem(y - d + 4, 4) * cols, 128)
        copies.append(pltpu.make_async_copy(w.at[:, pl.ds(first, cols)], w_all.at[d], sems.at[d]))
        copies[d].start()
    totals = [jnp.zeros((BLK, 2 * HD), jnp.float32)] * 2
    for d in range(4):
        copies[d].wait()
        both = jnp.concatenate([own[d], other[d]], axis=0)
        for half in range(2):
            totals[half] += nt_dot(both, w_all[d, half * 2 * HD : (half + 1) * 2 * HD])
    totals = [total.astype(jnp.bfloat16) for total in totals]
    for out, first in ((mine, z0 == 0), (theirs, z0 == 1)):
        for i, at in ((0, layer), (1, 1 - layer)):
            rows = slice(i * part, (i + 1) * part)
            out[pl.ds(pl.multiple_of(at * part, part), part), :] = jnp.where(first, totals[0][rows], totals[1][rows])


def dout(place, w, own, other):
    shape = jax.ShapeDtypeStruct((BLK, 2 * HD), jnp.bfloat16)
    return pl.pallas_call(
        dout_kernel,
        out_shape=(shape, shape),
        in_specs=[SM, HB, VM, VM],
        out_specs=(VM, VM),
        scratch_shapes=[pltpu.VMEM((4, w.shape[0], own.shape[2]), jnp.bfloat16), pltpu.SemaphoreType.DMA((4,))],
        name="dout",
        **params(16, 3),
    )(place, in_hbm(w), own, other)


def weigh(s):
    return jnp.exp2(jnp.tanh(s * TO_TANH) * TO_EXP2)


def expo_kernel(first, place, before, queries, near, far, expo, sums, acc, ahead):
    z1, z0, x, layer = place[0], place[1], place[2], place[3]
    acc[...] = jnp.zeros_like(acc)
    ahead[...] = lax.broadcasted_iota(jnp.int32, (BLK, BLK), 1) - lax.broadcasted_iota(jnp.int32, (BLK, BLK), 0)
    x_at = [lax.rem(x - d + NX, NX) for d in range(NX)]
    for e, keys in ((first, near), (first + 1, far)):

        def step(key_r, carry, e=e, keys=keys):
            kb = 2 * (e - first) + key_r
            k = keys[key_r]

            def work(r, mask):
                for d in range(NX):
                    for g in range(2):
                        ex = weigh(nt_dot(k, queries[d][r, :, g * HD : (g + 1) * HD]))
                        if mask is not None:
                            ex = jnp.where(mask(x_at[d]), ex, 0.0)
                        acc[g, d, r] += jnp.sum(ex.reshape(BLK // 8, 8, BLK), axis=0)
                        col = (g * 8 + d * 2 + r) * BLK
                        expo[kb, :, col : col + BLK] = ex.astype(jnp.bfloat16)

            def full():
                for r in range(2):
                    work(r, None)

            def mixed():
                for r in range(2):
                    apart = 2 * e + (z0 ^ r) - (z0 ^ key_r)
                    if e == 0:
                        all_kept, none_kept = apart > 0, apart < 0
                        mask = lambda at: ahead[...] >= (x - at) * BLK
                    else:
                        all_kept, none_kept = apart * BLK * NX < WINDOW, apart * BLK * NX > WINDOW
                        mask = lambda at: ahead[...] < (x - at) * BLK

                    @pl.when(all_kept)
                    def _(r=r):
                        work(r, None)

                    @pl.when(none_kept)
                    def _(r=r):
                        for d in range(NX):
                            for g in range(2):
                                col = (g * 8 + d * 2 + r) * BLK
                                expo[kb, :, col : col + BLK] = jnp.zeros((BLK, BLK), jnp.bfloat16)

                    @pl.when(jnp.logical_not(all_kept | none_kept))
                    def _(r=r, mask=mask):
                        work(r, mask)

            if e == 0:
                mixed()
            elif e == 2:
                pl.when(layer == 1)(full)
                pl.when(layer == 0)(mixed)
            else:
                full()
            return carry

        @pl.when(reached(e, z1, layer))
        def _(step=step):
            lax.fori_loop(0, 2, step, 0)

    for d in range(NX):
        for r in range(2):
            for g in range(2):
                row = r * 2 + g
                total = jnp.sum(acc[g, d, r], axis=0, keepdims=True)
                sums[x_at[d], row : row + 1, :] = total + before[x_at[d], row : row + 1, :]


def reached(e, z1, layer):
    return (e <= z1) & ((layer == 1) | (e * 2 - 1 <= WINDOW // (BLK * NX)))


def expo_call(first, place, before, queries, near, far):
    def kernel(place, before, q0, q1, q2, q3, *refs):
        expo_kernel(first, place, before, (q0, q1, q2, q3), *refs)

    return pl.pallas_call(
        kernel,
        out_shape=(
            pltpu.VMEM((4, BLK, 16 * BLK), jnp.bfloat16),
            jax.ShapeDtypeStruct((NX, 4, BLK), jnp.float32),
        ),
        in_specs=[SM] + [VM] * 7,
        out_specs=(VM, VM),
        scratch_shapes=[pltpu.VMEM((2, NX, 2, 8, BLK), jnp.float32), pltpu.VMEM((BLK, BLK), jnp.int32)],
        name=f"expo{first}",
        **params(10, 4),
    )(place, before, *queries, near, far)


def grads_kernel(place, expo0, expo2, *refs):
    grads, sums, outs, scaled = refs[0:4], refs[4:8], refs[8:12], refs[12]
    z1, x, layer = place[0], place[2], place[3]
    for d in range(NX):
        at = lax.rem(x - d + NX, NX)
        inverse = 1.0 / (sums[0][at] + sums[1][at] + sums[2][at] + sums[3][at])
        inverse = jnp.concatenate([inverse, inverse], axis=0).T
        for r in range(2):
            for g in range(2):
                piece = grads[d][r, :, g * HD : (g + 1) * HD].astype(jnp.float32)
                row = r * 2 + g
                col = (g * 8 + d * 2 + r) * BLK
                scaled[col : col + BLK] = (piece * inverse[:, row : row + 1]).astype(jnp.bfloat16)
    for e in range(4):
        used = reached(e, z1, layer)
        expo = (expo0, expo2)[e // 2]

        @pl.when(used)
        def _(e=e, expo=expo):
            for r in range(2):
                dots = jnp.dot(expo[e % 2 * 2 + r], scaled[...], preferred_element_type=jnp.float32)
                outs[e][r] = dots.astype(outs[e].dtype)

        @pl.when(jnp.logical_not(used))
        def _(e=e):
            outs[e][...] = jnp.zeros_like(outs[e])


def grads_call(place, expo0, expo2, grads, sums):
    far = jax.ShapeDtypeStruct((2, BLK, HD), jnp.bfloat16)
    return pl.pallas_call(
        grads_kernel,
        out_shape=(jax.ShapeDtypeStruct((2, BLK, HD), jnp.float32), far, far, far),
        in_specs=[SM] + [VM] * 10,
        out_specs=(VM,) * 4,
        scratch_shapes=[pltpu.VMEM((16 * BLK, HD), jnp.bfloat16)],
        name="value_grads",
        **params(12, 7),
    )(
        place,
        pltpu.with_memory_space_constraint(expo0, pltpu.VMEM),
        pltpu.with_memory_space_constraint(expo2, pltpu.VMEM),
        *grads,
        *sums,
    )


def contrib_kernel(place, v, w0, w1, w2, w3, gain, inv, out, sent):
    y = place[4]
    total = jnp.zeros(out.shape, jnp.float32)
    for d, w in enumerate((w0, w1, w2, w3)):
        at = lax.rem(y - d + 4, 4)
        total += nt_dot(jnp.concatenate([v[at], v[4 + at]], axis=1), w[...])
    total = total * gain[...] * inv[...]
    out[...] = total
    sent[...] = total.astype(sent.dtype)


def contrib_call(place, values, weights, gain, inv):
    cols = weights[0].shape[0]
    return pl.pallas_call(
        contrib_kernel,
        out_shape=(
            jax.ShapeDtypeStruct((BLK, cols), jnp.float32),
            jax.ShapeDtypeStruct((BLK, cols), jnp.bfloat16),
        ),
        in_specs=[SM] + [VM] * 7,
        out_specs=(VM, VM),
        name="contrib",
        **params(12, 2),
    )(place, values, *weights, gain, inv)


def edges_kernel(place, active, seed, contrib, higher, pool, resid, own, *far):
    y = place[4]
    resid[...] = (seed[...].astype(jnp.float32) + (higher[...].astype(jnp.float32) + contrib[...])).astype(jnp.bfloat16)
    for d in range(4):
        owner = lax.rem(y + d, 4)
        for t in range(2):
            rows = resid[t * TILE : (t + 1) * TILE, :]
            for k in range(2):
                slot = active[t, owner * 2 + k]
                dots = nt_dot(rows, pool[jnp.maximum(slot, 0)])
                dots = jnp.where(slot >= 0, dots, 0.0)
                if d == 0:
                    own[t, k] = dots
                else:
                    far[d - 1][t, k] = dots.astype(jnp.bfloat16)


def edges_call(place, active, seed, contrib, higher, pool):
    far = jax.ShapeDtypeStruct((2, 2, TILE, TILE), jnp.bfloat16)
    return pl.pallas_call(
        edges_kernel,
        out_shape=(
            jax.ShapeDtypeStruct(seed.shape, jnp.bfloat16),
            jax.ShapeDtypeStruct((2, 2, TILE, TILE), jnp.float32),
            far,
            far,
            far,
        ),
        in_specs=[SM, SM] + [VM] * 4,
        out_specs=(VM,) * 5,
        name="edges",
        **params(12, 3),
    )(place, active, seed, contrib, higher, pool)


def local(
    seed_grad,
    queries,
    key_cache,
    w_out,
    w_value,
    norm_gain,
    inv_rms,
    decoder_pool,
    active,
    feature_acts,
):
    z1, z0, x, y, layer = (lax.axis_index(a) for a in ("z1", "z0", "x", "head", "layer"))
    place = jnp.stack([z1, z0, x, layer, y]).astype(jnp.int32)
    cols = seed_grad.shape[1]
    half, q_mine, k_mine, qk_theirs, gain = parts_call(place, seed_grad, queries[0], key_cache[0], norm_gain)

    qk_from = rotate(qk_theirs, "z0", 1)
    q_pair = jnp.stack([q_mine, qk_from[:, : 2 * HD]])
    k_pair = jnp.stack([k_mine, qk_from[:, 2 * HD :]])
    k_all = [k_pair] + [along_pairs(k_pair, e, False) for e in (1, 2, 3)]
    q1, q2, q3 = (rotate(q_pair, "x", d) for d in (1, 2, 3))

    pieces = tuple(rotate(half, "head", d) for d in (1, 2, 3))
    pieces = lax.optimization_barrier(pieces + (k_pair, q1, q3))[:3]
    halves = jnp.stack((half,) + pieces)
    w_rows = rows_call(place, after(w_value[0], *pieces))
    others = after(rotate(halves, "layer", 1), q2)
    d_mine, d_theirs = dout(place, w_out[0], halves, others)
    d_pair = jnp.stack([d_mine, rotate(d_theirs, "z0", 1)])
    grads = [d_pair] + [rotate(d_pair, "x", d) for d in (1, 2, 3)]
    w_cols = [w_rows[0]] + [rotate(after(w_rows[d], d_pair), "head", d) for d in (1, 2, 3)]

    none = jnp.zeros((NX, 4, BLK), jnp.float32)
    q_all = (q_pair, q1, q2, q3)
    expo0, sums = expo_call(0, place, none, q_all, k_all[0], k_all[1])
    expo2, sums = expo_call(2, place, sums, q_all, k_all[2], k_all[3])
    sums = [sums] + [rotate(sums, "x", d) for d in (1, 2, 3)]

    near, *far = grads_call(place, expo0, expo2, grads, sums)
    far = [along_pairs(far[e - 1], e, True) for e in (1, 2, 3)]
    totals = total_call(place, after(near, *w_cols[1:]), far)
    values = lax.all_to_all(totals, ("z0", "head"), 0, 0, tiled=True)
    contrib, sent = contrib_call(place, values, w_cols, gain, inv_rms.reshape(BLK, 1))
    higher = lax.ppermute(sent, "layer", [(1, 0)])
    resid, mine, *parts = edges_call(place, active[0], seed_grad, contrib, higher, decoder_pool[0])
    for d in (1, 2, 3):
        mine = mine + rotate(parts[d - 1], "head", d).astype(jnp.float32)
    edges = (mine * feature_acts[0].astype(jnp.float32)).astype(jnp.bfloat16)
    return edges[None], resid[None]


def solution(mesh):
    fine = Mesh(mesh.devices.reshape(2, NP, 2, NX, 4), ("layer", "z1", "z0", "x", "head"))
    seq = ("z1", "z0", "x")
    placed = (
        P(seq, "head"),
        P("layer", seq, "head"),
        P("layer", seq, "head"),
        P("layer", "head", None),
        P("layer", None, "head"),
        P("layer", None),
        P("layer", seq),
        P("layer", None, None, "head"),
        P("layer", seq, None),
        P("layer", seq, "head", None, None),
    )
    return jax.shard_map(
        local,
        mesh=fine,
        in_specs=placed,
        out_specs=(P("layer", seq, "head", None, None), P("layer", seq, "head")),
        check_vma=False,
    )
```

```python
import functools
import math

import jax
import jax.numpy as jnp
from jax import lax
from jax.experimental import pallas as pl
from jax.experimental.pallas import tpu as pltpu
from jax.sharding import Mesh, PartitionSpec as P

HD = 128
TILE = 128
WINDOW = 4096
SOFTCAP = 50.0
TO_TANH = 1.0 / 12.0 / SOFTCAP
TO_EXP2 = SOFTCAP * math.log2(math.e)

NX = 4
NP = 4
BLK = 256


def rotate(a, axis, d):
    n = lax.axis_size(axis)
    return lax.ppermute(a, axis, [(i, (i + d) % n) for i in range(n)])


def along_pairs(a, e, back):
    pairs = []
    for layer in range(2):
        for z1 in range(NP - e):
            near, far = layer * NP + z1, layer * NP + z1 + e
            if layer == 1 or e * 2 - 1 <= WINDOW // (BLK * NX):
                pairs.append((far, near) if back else (near, far))
    return lax.ppermute(a, ("layer", "z1"), pairs)


def after(a, *others):
    return lax.optimization_barrier((a,) + others)[0]


def nt_dot(a, b):
    return lax.dot_general(a, b, (((1,), (1,)), ((), ())), preferred_element_type=jnp.float32)


VM = pl.BlockSpec(memory_space=pltpu.VMEM)
SM = pl.BlockSpec(memory_space=pltpu.SMEM)
HB = pl.BlockSpec(memory_space=pltpu.HBM)


def in_hbm(a):
    return pltpu.with_memory_space_constraint(a, pltpu.HBM)


def params(mib, us):
    return dict(
        compiler_params=pltpu.CompilerParams(vmem_limit_bytes=mib * 1024 * 1024),
        cost_estimate=pl.CostEstimate(flops=int(us * 1e9), bytes_accessed=0, transcendentals=0),
    )


def parts_kernel(place, seed, q, k, gain, half, q_mine, k_mine, qk_theirs, gain_cols, sems):
    z0, layer, y = place[1], place[3], place[4]
    cols = half.shape[1]
    moves = (
        (seed.at[pl.ds(pl.multiple_of(layer * (BLK // 2), BLK // 2), BLK // 2), :], half),
        (q.at[:, pl.ds(pl.multiple_of((1 - z0) * 2 * HD, 2 * HD), 2 * HD)], qk_theirs.at[:, : 2 * HD]),
        (k.at[:, pl.ds(pl.multiple_of((1 - z0) * HD, HD), HD)], qk_theirs.at[:, 2 * HD :]),
        (q.at[:, pl.ds(pl.multiple_of(z0 * 2 * HD, 2 * HD), 2 * HD)], q_mine),
        (k.at[:, pl.ds(pl.multiple_of(z0 * HD, HD), HD)], k_mine),
        (gain.at[:, pl.ds(pl.multiple_of(y * cols, 128), cols)], gain_cols),
    )
    copies = [pltpu.make_async_copy(a, b, sems.at[i]) for i, (a, b) in enumerate(moves)]
    for copy in copies:
        copy.start()
    for copy in copies:
        copy.wait()


def parts_call(place, seed, q, k, gain):
    cols = seed.shape[1]
    b16 = jnp.bfloat16
    return pl.pallas_call(
        parts_kernel,
        out_shape=(
            jax.ShapeDtypeStruct((BLK // 2, cols), b16),
            jax.ShapeDtypeStruct((BLK, 2 * HD), b16),
            jax.ShapeDtypeStruct((BLK, HD), b16),
            jax.ShapeDtypeStruct((BLK, 3 * HD), b16),
            jax.ShapeDtypeStruct((1, cols), jnp.float32),
        ),
        in_specs=[SM] + [HB] * 4,
        out_specs=(VM,) * 5,
        scratch_shapes=[pltpu.SemaphoreType.DMA((6,))],
        name="parts",
        **params(8, 1),
    )(place, in_hbm(seed), in_hbm(q), in_hbm(k), in_hbm(gain))


def rows_kernel(place, w, *refs):
    outs, sems = refs[:4], refs[4]
    y = place[4]
    cols = outs[0].shape[0]
    copies = []
    for d, out in enumerate(outs):
        rows = pl.ds(pl.multiple_of(lax.rem(y + d, 4) * cols, 128), cols)
        copies.append(pltpu.make_async_copy(w.at[rows, :], out, sems.at[d]))
        copies[d].start()
    for copy in copies:
        copy.wait()


def rows_call(place, w):
    shape = jax.ShapeDtypeStruct((w.shape[0] // 4, w.shape[1]), w.dtype)
    return pl.pallas_call(
        rows_kernel,
        out_shape=(shape,) * 4,
        in_specs=[SM, HB],
        out_specs=(VM,) * 4,
        scratch_shapes=[pltpu.SemaphoreType.DMA((4,))],
        name="rows",
        **params(12, 1),
    )(place, in_hbm(w))


def total_kernel(place, near, far0, far1, far2, mine, theirs):
    for r, out in ((1, theirs), (0, mine)):
        total = near[r]
        for far in (far0, far1, far2):
            total += far[r].astype(jnp.float32)
        out[...] = total.astype(out.dtype)


def total_call(place, near, far):
    shape = jax.ShapeDtypeStruct((BLK, HD), jnp.bfloat16)
    return pl.pallas_call(
        total_kernel,
        out_shape=(shape, shape),
        in_specs=[SM] + [VM] * 4,
        out_specs=(VM, VM),
        name="total",
        **params(8, 1),
    )(place, near, *far)


def dout_kernel(place, w, own, other, mine, theirs):
    z0, layer, y = place[1], place[3], place[4]
    cols = own.shape[2]
    part = BLK // 2
    for out, half in ((theirs, 1 - z0), (mine, z0)):
        rows = pl.ds(pl.multiple_of(half * 2 * HD, 2 * HD), 2 * HD)
        total = jnp.zeros((BLK, 2 * HD), jnp.float32)
        for d in range(4):
            first = pl.multiple_of(lax.rem(y - d + 4, 4) * cols, 128)
            both = jnp.concatenate([own[d], other[d]], axis=0)
            total += nt_dot(both, w[rows, pl.ds(first, cols)])
        total = total.astype(jnp.bfloat16)
        out[pl.ds(pl.multiple_of(layer * part, part), part), :] = total[:part]
        out[pl.ds(pl.multiple_of((1 - layer) * part, part), part), :] = total[part:]


def dout(place, w, own, other):
    shape = jax.ShapeDtypeStruct((BLK, 2 * HD), jnp.bfloat16)
    return pl.pallas_call(
        dout_kernel,
        out_shape=(shape, shape),
        in_specs=[SM, VM, VM, VM],
        out_specs=(VM, VM),
        name="dout",
        **params(16, 3),
    )(place, w, own, other)


def weigh(s):
    return jnp.exp2(jnp.tanh(s * TO_TANH) * TO_EXP2)


def expo_kernel(first, place, before, queries, near, far, expo, sums, acc, ahead):
    z1, z0, x, layer = place[0], place[1], place[2], place[3]
    acc[...] = jnp.zeros_like(acc)
    ahead[...] = lax.broadcasted_iota(jnp.int32, (BLK, BLK), 1) - lax.broadcasted_iota(jnp.int32, (BLK, BLK), 0)
    x_at = [lax.rem(x - d + NX, NX) for d in range(NX)]
    for e, keys in ((first, near), (first + 1, far)):

        def step(key_r, carry, e=e, keys=keys):
            kb = 2 * (e - first) + key_r
            k = keys[key_r]

            def work(r, mask):
                for d in range(NX):
                    for g in range(2):
                        ex = weigh(nt_dot(k, queries[d][r, :, g * HD : (g + 1) * HD]))
                        if mask is not None:
                            ex = jnp.where(mask(x_at[d]), ex, 0.0)
                        acc[g, d, r] += jnp.sum(ex.reshape(BLK // 8, 8, BLK), axis=0)
                        col = (g * 8 + d * 2 + r) * BLK
                        expo[kb, :, col : col + BLK] = ex.astype(jnp.bfloat16)

            def full():
                for r in range(2):
                    work(r, None)

            def mixed():
                for r in range(2):
                    apart = 2 * e + (z0 ^ r) - (z0 ^ key_r)
                    if e == 0:
                        all_kept, none_kept = apart > 0, apart < 0
                        mask = lambda at: ahead[...] >= (x - at) * BLK
                    else:
                        all_kept, none_kept = apart * BLK * NX < WINDOW, apart * BLK * NX > WINDOW
                        mask = lambda at: ahead[...] < (x - at) * BLK

                    @pl.when(all_kept)
                    def _(r=r):
                        work(r, None)

                    @pl.when(none_kept)
                    def _(r=r):
                        for d in range(NX):
                            for g in range(2):
                                col = (g * 8 + d * 2 + r) * BLK
                                expo[kb, :, col : col + BLK] = jnp.zeros((BLK, BLK), jnp.bfloat16)

                    @pl.when(jnp.logical_not(all_kept | none_kept))
                    def _(r=r, mask=mask):
                        work(r, mask)

            if e == 0:
                mixed()
            elif e == 2:
                pl.when(layer == 1)(full)
                pl.when(layer == 0)(mixed)
            else:
                full()
            return carry

        @pl.when(reached(e, z1, layer))
        def _(step=step):
            lax.fori_loop(0, 2, step, 0)

    for d in range(NX):
        for r in range(2):
            for g in range(2):
                row = r * 2 + g
                total = jnp.sum(acc[g, d, r], axis=0, keepdims=True)
                sums[x_at[d], row : row + 1, :] = total + before[x_at[d], row : row + 1, :]


def reached(e, z1, layer):
    return (e <= z1) & ((layer == 1) | (e * 2 - 1 <= WINDOW // (BLK * NX)))


def expo_call(first, place, before, queries, near, far):
    def kernel(place, before, q0, q1, q2, q3, *refs):
        expo_kernel(first, place, before, (q0, q1, q2, q3), *refs)

    return pl.pallas_call(
        kernel,
        out_shape=(
            pltpu.VMEM((4, BLK, 16 * BLK), jnp.bfloat16),
            jax.ShapeDtypeStruct((NX, 4, BLK), jnp.float32),
        ),
        in_specs=[SM] + [VM] * 7,
        out_specs=(VM, VM),
        scratch_shapes=[pltpu.VMEM((2, NX, 2, 8, BLK), jnp.float32), pltpu.VMEM((BLK, BLK), jnp.int32)],
        name=f"expo{first}",
        **params(10, 4),
    )(place, before, *queries, near, far)


def grads_kernel(place, expo0, expo2, *refs):
    grads, sums, outs, scaled = refs[0:4], refs[4:8], refs[8:12], refs[12]
    z1, x, layer = place[0], place[2], place[3]
    for d in range(NX):
        at = lax.rem(x - d + NX, NX)
        inverse = 1.0 / (sums[0][at] + sums[1][at] + sums[2][at] + sums[3][at])
        inverse = jnp.concatenate([inverse, inverse], axis=0).T
        for r in range(2):
            for g in range(2):
                piece = grads[d][r, :, g * HD : (g + 1) * HD].astype(jnp.float32)
                row = r * 2 + g
                col = (g * 8 + d * 2 + r) * BLK
                scaled[col : col + BLK] = (piece * inverse[:, row : row + 1]).astype(jnp.bfloat16)
    for e in range(4):
        used = reached(e, z1, layer)
        expo = (expo0, expo2)[e // 2]

        @pl.when(used)
        def _(e=e, expo=expo):
            for r in range(2):
                dots = jnp.dot(expo[e % 2 * 2 + r], scaled[...], preferred_element_type=jnp.float32)
                outs[e][r] = dots.astype(outs[e].dtype)

        @pl.when(jnp.logical_not(used))
        def _(e=e):
            outs[e][...] = jnp.zeros_like(outs[e])


def grads_call(place, expo0, expo2, grads, sums):
    far = jax.ShapeDtypeStruct((2, BLK, HD), jnp.bfloat16)
    return pl.pallas_call(
        grads_kernel,
        out_shape=(jax.ShapeDtypeStruct((2, BLK, HD), jnp.float32), far, far, far),
        in_specs=[SM] + [VM] * 10,
        out_specs=(VM,) * 4,
        scratch_shapes=[pltpu.VMEM((16 * BLK, HD), jnp.bfloat16)],
        name="value_grads",
        **params(12, 7),
    )(
        place,
        pltpu.with_memory_space_constraint(expo0, pltpu.VMEM),
        pltpu.with_memory_space_constraint(expo2, pltpu.VMEM),
        *grads,
        *sums,
    )


def contrib_kernel(place, v0, v1, v2, v3, w0, w1, w2, w3, gain, inv, out, sent):
    z0 = place[1]
    total = jnp.zeros(out.shape, jnp.float32)
    for v, w in ((v0, w0), (v1, w1), (v2, w2), (v3, w3)):
        total += nt_dot(jnp.concatenate([v[z0], v[1 - z0]], axis=1), w[...])
    total = total * gain[...] * inv[...]
    out[...] = total
    sent[...] = total.astype(sent.dtype)


def contrib_call(place, values, weights, gain, inv):
    cols = weights[0].shape[0]
    return pl.pallas_call(
        contrib_kernel,
        out_shape=(
            jax.ShapeDtypeStruct((BLK, cols), jnp.float32),
            jax.ShapeDtypeStruct((BLK, cols), jnp.bfloat16),
        ),
        in_specs=[SM] + [VM] * 10,
        out_specs=(VM, VM),
        name="contrib",
        **params(12, 2),
    )(place, *values, *weights, gain, inv)


def edges_kernel(place, active, seed, contrib, higher, pool, resid, own, *far):
    y = place[4]
    resid[...] = (seed[...].astype(jnp.float32) + (higher[...].astype(jnp.float32) + contrib[...])).astype(jnp.bfloat16)
    for d in range(4):
        owner = lax.rem(y + d, 4)
        for t in range(2):
            rows = resid[t * TILE : (t + 1) * TILE, :]
            for k in range(2):
                slot = active[t, owner * 2 + k]
                dots = nt_dot(rows, pool[jnp.maximum(slot, 0)])
                dots = jnp.where(slot >= 0, dots, 0.0)
                if d == 0:
                    own[t, k] = dots
                else:
                    far[d - 1][t, k] = dots.astype(jnp.bfloat16)


def edges_call(place, active, seed, contrib, higher, pool):
    far = jax.ShapeDtypeStruct((2, 2, TILE, TILE), jnp.bfloat16)
    return pl.pallas_call(
        edges_kernel,
        out_shape=(
            jax.ShapeDtypeStruct(seed.shape, jnp.bfloat16),
            jax.ShapeDtypeStruct((2, 2, TILE, TILE), jnp.float32),
            far,
            far,
            far,
        ),
        in_specs=[SM, SM] + [VM] * 4,
        out_specs=(VM,) * 5,
        name="edges",
        **params(12, 3),
    )(place, active, seed, contrib, higher, pool)


def local(
    seed_grad,
    queries,
    key_cache,
    w_out,
    w_value,
    norm_gain,
    inv_rms,
    decoder_pool,
    active,
    feature_acts,
):
    z1, z0, x, y, layer = (lax.axis_index(a) for a in ("z1", "z0", "x", "head", "layer"))
    place = jnp.stack([z1, z0, x, layer, y]).astype(jnp.int32)
    cols = seed_grad.shape[1]
    half, q_mine, k_mine, qk_theirs, gain = parts_call(place, seed_grad, queries[0], key_cache[0], norm_gain)

    qk_from = rotate(qk_theirs, "z0", 1)
    q_pair = jnp.stack([q_mine, qk_from[:, : 2 * HD]])
    k_pair = jnp.stack([k_mine, qk_from[:, 2 * HD :]])
    q1, q2, q3 = (rotate(q_pair, "x", d) for d in (1, 2, 3))

    pieces = tuple(rotate(half, "head", d) for d in (1, 2, 3))
    w_rows = rows_call(place, after(w_value[0], k_pair))
    *pieces, k_pair, q1, q3, w0, w1, w2, w3 = lax.optimization_barrier(pieces + (k_pair, q1, q3) + tuple(w_rows))
    halves = jnp.stack([half] + pieces)
    d_mine, d_theirs = dout(place, w_out[0], halves, rotate(halves, "layer", 1))
    d_pair = jnp.stack([d_mine, rotate(d_theirs, "z0", 1)])
    grads = [d_pair] + [rotate(d_pair, "x", d) for d in (1, 2, 3)]
    k_pair = after(k_pair, d_mine)
    k_all = [k_pair] + [rotate(k_pair, "z1", e) for e in (1, 2, 3)]
    w1, w3 = rotate(after(w1, d_mine), "head", 1), rotate(after(w3, d_mine), "head", 3)
    w2 = rotate(after(w2, w1, w3), "head", 2)

    none = jnp.zeros((NX, 4, BLK), jnp.float32)
    q_all = (q_pair, q1, q2, q3)
    expo0, sums = expo_call(0, place, none, q_all, k_all[0], k_all[1])
    expo2, sums = expo_call(2, place, sums, q_all, k_all[2], k_all[3])
    sums = after(sums, w1, w3)
    sums = [sums] + [rotate(sums, "x", d) for d in (1, 2, 3)]

    near, *far = grads_call(place, expo0, expo2, grads, sums)
    far = [along_pairs(far[e - 1], e, True) for e in (1, 2, 3)]
    mine, theirs = total_call(place, after(near, w2), far)
    v_pair = jnp.stack([mine, rotate(theirs, "z0", 1)])
    values = [v_pair] + [rotate(v_pair, "head", d) for d in (1, 2, 3)]
    contrib, sent = contrib_call(place, values, (w0, w1, w2, w3), gain, inv_rms.reshape(BLK, 1))
    higher = lax.ppermute(sent, "layer", [(1, 0)])
    resid, mine, *parts = edges_call(place, active[0], seed_grad, contrib, higher, decoder_pool[0])
    for d in (1, 2, 3):
        mine = mine + rotate(parts[d - 1], "head", d).astype(jnp.float32)
    edges = (mine * feature_acts[0].astype(jnp.float32)).astype(jnp.bfloat16)
    return edges[None], resid[None]


def solution(mesh):
    fine = Mesh(mesh.devices.reshape(2, NP, 2, NX, 4), ("layer", "z1", "z0", "x", "head"))
    seq = ("z1", "z0", "x")
    placed = (
        P(seq, "head"),
        P("layer", seq, "head"),
        P("layer", seq, "head"),
        P("layer", "head", None),
        P("layer", None, "head"),
        P("layer", None),
        P("layer", seq),
        P("layer", None, None, "head"),
        P("layer", seq, None),
        P("layer", seq, "head", None, None),
    )
    return jax.shard_map(
        local,
        mesh=fine,
        in_specs=placed,
        out_specs=(P("layer", seq, "head", None, None), P("layer", seq, "head")),
        check_vma=False,
    )
```

```python
import functools
import math

import jax
import jax.numpy as jnp
from jax import lax
from jax.experimental import pallas as pl
from jax.experimental.pallas import tpu as pltpu
from jax.sharding import Mesh, PartitionSpec as P

HD = 128
TILE = 128
WINDOW = 4096
SOFTCAP = 50.0
TO_TANH = 1.0 / 12.0 / SOFTCAP
TO_EXP2 = SOFTCAP * math.log2(math.e)

NX = 4
NP = 4
BLK = 256


def rotate(a, axis, d):
    n = lax.axis_size(axis)
    return lax.ppermute(a, axis, [(i, (i + d) % n) for i in range(n)])


def along_pairs(a, e, back):
    pairs = []
    for layer in range(2):
        for z1 in range(NP - e):
            near, far = layer * NP + z1, layer * NP + z1 + e
            if layer == 1 or e * 2 - 1 <= WINDOW // (BLK * NX):
                pairs.append((far, near) if back else (near, far))
    return lax.ppermute(a, ("layer", "z1"), pairs)


def after(a, *others):
    return lax.optimization_barrier((a,) + others)[0]


def nt_dot(a, b):
    return lax.dot_general(a, b, (((1,), (1,)), ((), ())), preferred_element_type=jnp.float32)


VM = pl.BlockSpec(memory_space=pltpu.VMEM)
SM = pl.BlockSpec(memory_space=pltpu.SMEM)
HB = pl.BlockSpec(memory_space=pltpu.HBM)


def in_hbm(a):
    return pltpu.with_memory_space_constraint(a, pltpu.HBM)


def params(mib, us):
    return dict(
        compiler_params=pltpu.CompilerParams(vmem_limit_bytes=mib * 1024 * 1024),
        cost_estimate=pl.CostEstimate(flops=int(us * 1e9), bytes_accessed=0, transcendentals=0),
    )


def parts_kernel(place, seed, q, k, gain, half, q_mine, k_mine, qk_theirs, gain_cols, sems):
    z0, layer, y = place[1], place[3], place[4]
    cols = half.shape[1]
    moves = (
        (seed.at[pl.ds(pl.multiple_of(layer * (BLK // 2), BLK // 2), BLK // 2), :], half),
        (q.at[:, pl.ds(pl.multiple_of((1 - z0) * 2 * HD, 2 * HD), 2 * HD)], qk_theirs.at[:, : 2 * HD]),
        (k.at[:, pl.ds(pl.multiple_of((1 - z0) * HD, HD), HD)], qk_theirs.at[:, 2 * HD :]),
        (q.at[:, pl.ds(pl.multiple_of(z0 * 2 * HD, 2 * HD), 2 * HD)], q_mine),
        (k.at[:, pl.ds(pl.multiple_of(z0 * HD, HD), HD)], k_mine),
        (gain.at[:, pl.ds(pl.multiple_of(y * cols, 128), cols)], gain_cols),
    )
    copies = [pltpu.make_async_copy(a, b, sems.at[i]) for i, (a, b) in enumerate(moves)]
    for copy in copies:
        copy.start()
    for copy in copies:
        copy.wait()


def parts_call(place, seed, q, k, gain):
    cols = seed.shape[1]
    b16 = jnp.bfloat16
    return pl.pallas_call(
        parts_kernel,
        out_shape=(
            jax.ShapeDtypeStruct((BLK // 2, cols), b16),
            jax.ShapeDtypeStruct((BLK, 2 * HD), b16),
            jax.ShapeDtypeStruct((BLK, HD), b16),
            jax.ShapeDtypeStruct((BLK, 3 * HD), b16),
            jax.ShapeDtypeStruct((1, cols), jnp.float32),
        ),
        in_specs=[SM] + [HB] * 4,
        out_specs=(VM,) * 5,
        scratch_shapes=[pltpu.SemaphoreType.DMA((6,))],
        name="parts",
        **params(8, 1),
    )(place, in_hbm(seed), in_hbm(q), in_hbm(k), in_hbm(gain))


def rows_kernel(place, w, *refs):
    outs, sems = refs[:4], refs[4]
    y = place[4]
    cols = outs[0].shape[0]
    copies = []
    for d, out in enumerate(outs):
        rows = pl.ds(pl.multiple_of(lax.rem(y + d, 4) * cols, 128), cols)
        copies.append(pltpu.make_async_copy(w.at[rows, :], out, sems.at[d]))
        copies[d].start()
    for copy in copies:
        copy.wait()


def rows_call(place, w):
    shape = jax.ShapeDtypeStruct((w.shape[0] // 4, w.shape[1]), w.dtype)
    return pl.pallas_call(
        rows_kernel,
        out_shape=(shape,) * 4,
        in_specs=[SM, HB],
        out_specs=(VM,) * 4,
        scratch_shapes=[pltpu.SemaphoreType.DMA((4,))],
        name="rows",
        **params(12, 1),
    )(place, in_hbm(w))


def total_kernel(place, near, far0, far1, far2, mine, theirs):
    for r, out in ((1, theirs), (0, mine)):
        total = near[r]
        for far in (far0, far1, far2):
            total += far[r].astype(jnp.float32)
        out[...] = total.astype(out.dtype)


def total_call(place, near, far):
    shape = jax.ShapeDtypeStruct((BLK, HD), jnp.bfloat16)
    return pl.pallas_call(
        total_kernel,
        out_shape=(shape, shape),
        in_specs=[SM] + [VM] * 4,
        out_specs=(VM, VM),
        name="total",
        **params(8, 1),
    )(place, near, *far)


def dout_kernel(place, w, own, other, mine, theirs):
    z0, layer, y = place[1], place[3], place[4]
    cols = own.shape[2]
    part = BLK // 2
    for out, half in ((theirs, 1 - z0), (mine, z0)):
        rows = pl.ds(pl.multiple_of(half * 2 * HD, 2 * HD), 2 * HD)
        total = jnp.zeros((BLK, 2 * HD), jnp.float32)
        for d in range(4):
            first = pl.multiple_of(lax.rem(y - d + 4, 4) * cols, 128)
            both = jnp.concatenate([own[d], other[d]], axis=0)
            total += nt_dot(both, w[rows, pl.ds(first, cols)])
        total = total.astype(jnp.bfloat16)
        out[pl.ds(pl.multiple_of(layer * part, part), part), :] = total[:part]
        out[pl.ds(pl.multiple_of((1 - layer) * part, part), part), :] = total[part:]


def dout(place, w, own, other):
    shape = jax.ShapeDtypeStruct((BLK, 2 * HD), jnp.bfloat16)
    return pl.pallas_call(
        dout_kernel,
        out_shape=(shape, shape),
        in_specs=[SM, VM, VM, VM],
        out_specs=(VM, VM),
        name="dout",
        **params(16, 3),
    )(place, w, own, other)


def weigh(s):
    return jnp.exp2(jnp.tanh(s * TO_TANH) * TO_EXP2)


def expo_kernel(first, place, before, queries, near, far, expo, sums, acc, ahead):
    z1, z0, x, layer = place[0], place[1], place[2], place[3]
    acc[...] = jnp.zeros_like(acc)
    ahead[...] = lax.broadcasted_iota(jnp.int32, (BLK, BLK), 1) - lax.broadcasted_iota(jnp.int32, (BLK, BLK), 0)
    x_at = [lax.rem(x - d + NX, NX) for d in range(NX)]
    for e, keys in ((first, near), (first + 1, far)):

        def step(key_r, carry, e=e, keys=keys):
            kb = 2 * (e - first) + key_r
            k = keys[key_r]

            def work(r, mask):
                for d in range(NX):
                    for g in range(2):
                        ex = weigh(nt_dot(k, queries[d][r, :, g * HD : (g + 1) * HD]))
                        if mask is not None:
                            ex = jnp.where(mask(x_at[d]), ex, 0.0)
                        acc[g, d, r] += jnp.sum(ex.reshape(BLK // 8, 8, BLK), axis=0)
                        col = pl.multiple_of((g * 8 + d * 2 + r) * BLK, BLK)
                        expo[kb, :, pl.ds(col, BLK)] = ex.astype(jnp.bfloat16)

            def full():
                def one(r, carry):
                    work(r, None)
                    return carry

                lax.fori_loop(0, 2, one, 0)

            def mixed():
                def one(r, carry):
                    apart = 2 * e + (z0 ^ r) - (z0 ^ key_r)
                    if e == 0:
                        all_kept, none_kept = apart > 0, apart < 0
                        mask = lambda at: ahead[...] >= (x - at) * BLK
                    else:
                        all_kept, none_kept = apart * BLK * NX < WINDOW, apart * BLK * NX > WINDOW
                        mask = lambda at: ahead[...] < (x - at) * BLK

                    @pl.when(all_kept)
                    def _():
                        work(r, None)

                    @pl.when(none_kept)
                    def _():
                        for d in range(NX):
                            for g in range(2):
                                col = pl.multiple_of((g * 8 + d * 2 + r) * BLK, BLK)
                                expo[kb, :, pl.ds(col, BLK)] = jnp.zeros((BLK, BLK), jnp.bfloat16)

                    @pl.when(jnp.logical_not(all_kept | none_kept))
                    def _():
                        work(r, mask)

                    return carry

                lax.fori_loop(0, 2, one, 0)

            if e == 0:
                mixed()
            elif e == 2:
                pl.when(layer == 1)(full)
                pl.when(layer == 0)(mixed)
            else:
                full()
            return carry

        @pl.when(reached(e, z1, layer))
        def _(step=step):
            lax.fori_loop(0, 2, step, 0)

    for d in range(NX):
        for r in range(2):
            for g in range(2):
                row = r * 2 + g
                total = jnp.sum(acc[g, d, r], axis=0, keepdims=True)
                sums[x_at[d], row : row + 1, :] = total + before[x_at[d], row : row + 1, :]


def reached(e, z1, layer):
    return (e <= z1) & ((layer == 1) | (e * 2 - 1 <= WINDOW // (BLK * NX)))


def expo_call(first, place, before, queries, near, far):
    def kernel(place, before, q0, q1, q2, q3, *refs):
        expo_kernel(first, place, before, (q0, q1, q2, q3), *refs)

    return pl.pallas_call(
        kernel,
        out_shape=(
            pltpu.VMEM((4, BLK, 16 * BLK), jnp.bfloat16),
            jax.ShapeDtypeStruct((NX, 4, BLK), jnp.float32),
        ),
        in_specs=[SM] + [VM] * 7,
        out_specs=(VM, VM),
        scratch_shapes=[pltpu.VMEM((2, NX, 2, 8, BLK), jnp.float32), pltpu.VMEM((BLK, BLK), jnp.int32)],
        name=f"expo{first}",
        **params(10, 4),
    )(place, before, *queries, near, far)


def grads_kernel(place, expo0, expo2, *refs):
    grads, sums, outs, scaled = refs[0:4], refs[4:8], refs[8:12], refs[12]
    z1, x, layer = place[0], place[2], place[3]
    for d in range(NX):
        at = lax.rem(x - d + NX, NX)
        inverse = 1.0 / (sums[0][at] + sums[1][at] + sums[2][at] + sums[3][at])
        inverse = jnp.concatenate([inverse, inverse], axis=0).T
        for r in range(2):
            for g in range(2):
                piece = grads[d][r, :, g * HD : (g + 1) * HD].astype(jnp.float32)
                row = r * 2 + g
                col = (g * 8 + d * 2 + r) * BLK
                scaled[col : col + BLK] = (piece * inverse[:, row : row + 1]).astype(jnp.bfloat16)
    for e in range(4):
        used = reached(e, z1, layer)
        expo = (expo0, expo2)[e // 2]

        @pl.when(used)
        def _(e=e, expo=expo):
            for r in range(2):
                dots = jnp.dot(expo[e % 2 * 2 + r], scaled[...], preferred_element_type=jnp.float32)
                outs[e][r] = dots.astype(outs[e].dtype)

        @pl.when(jnp.logical_not(used))
        def _(e=e):
            outs[e][...] = jnp.zeros_like(outs[e])


def grads_call(place, expo0, expo2, grads, sums):
    far = jax.ShapeDtypeStruct((2, BLK, HD), jnp.bfloat16)
    return pl.pallas_call(
        grads_kernel,
        out_shape=(jax.ShapeDtypeStruct((2, BLK, HD), jnp.float32), far, far, far),
        in_specs=[SM] + [VM] * 10,
        out_specs=(VM,) * 4,
        scratch_shapes=[pltpu.VMEM((16 * BLK, HD), jnp.bfloat16)],
        name="value_grads",
        **params(12, 7),
    )(
        place,
        pltpu.with_memory_space_constraint(expo0, pltpu.VMEM),
        pltpu.with_memory_space_constraint(expo2, pltpu.VMEM),
        *grads,
        *sums,
    )


def contrib_kernel(place, v0, v1, v2, v3, w0, w1, w2, w3, gain, inv, out, sent):
    z0 = place[1]
    total = jnp.zeros(out.shape, jnp.float32)
    for v, w in ((v0, w0), (v1, w1), (v2, w2), (v3, w3)):
        total += nt_dot(jnp.concatenate([v[z0], v[1 - z0]], axis=1), w[...])
    total = total * gain[...] * inv[...]
    out[...] = total
    sent[...] = total.astype(sent.dtype)


def contrib_call(place, values, weights, gain, inv):
    cols = weights[0].shape[0]
    return pl.pallas_call(
        contrib_kernel,
        out_shape=(
            jax.ShapeDtypeStruct((BLK, cols), jnp.float32),
            jax.ShapeDtypeStruct((BLK, cols), jnp.bfloat16),
        ),
        in_specs=[SM] + [VM] * 10,
        out_specs=(VM, VM),
        name="contrib",
        **params(12, 2),
    )(place, *values, *weights, gain, inv)


def edges_kernel(place, active, seed, contrib, higher, pool, resid, own, *far):
    y = place[4]
    resid[...] = (seed[...].astype(jnp.float32) + (higher[...].astype(jnp.float32) + contrib[...])).astype(jnp.bfloat16)
    for d in range(4):
        owner = lax.rem(y + d, 4)
        for t in range(2):
            rows = resid[t * TILE : (t + 1) * TILE, :]
            for k in range(2):
                slot = active[t, owner * 2 + k]
                dots = nt_dot(rows, pool[jnp.maximum(slot, 0)])
                dots = jnp.where(slot >= 0, dots, 0.0)
                if d == 0:
                    own[t, k] = dots
                else:
                    far[d - 1][t, k] = dots.astype(jnp.bfloat16)


def edges_call(place, active, seed, contrib, higher, pool):
    far = jax.ShapeDtypeStruct((2, 2, TILE, TILE), jnp.bfloat16)
    return pl.pallas_call(
        edges_kernel,
        out_shape=(
            jax.ShapeDtypeStruct(seed.shape, jnp.bfloat16),
            jax.ShapeDtypeStruct((2, 2, TILE, TILE), jnp.float32),
            far,
            far,
            far,
        ),
        in_specs=[SM, SM] + [VM] * 4,
        out_specs=(VM,) * 5,
        name="edges",
        **params(12, 3),
    )(place, active, seed, contrib, higher, pool)


def local(
    seed_grad,
    queries,
    key_cache,
    w_out,
    w_value,
    norm_gain,
    inv_rms,
    decoder_pool,
    active,
    feature_acts,
):
    z1, z0, x, y, layer = (lax.axis_index(a) for a in ("z1", "z0", "x", "head", "layer"))
    place = jnp.stack([z1, z0, x, layer, y]).astype(jnp.int32)
    cols = seed_grad.shape[1]
    half, q_mine, k_mine, qk_theirs, gain = parts_call(place, seed_grad, queries[0], key_cache[0], norm_gain)

    qk_from = rotate(qk_theirs, "z0", 1)
    q_pair = jnp.stack([q_mine, qk_from[:, : 2 * HD]])
    k_pair = jnp.stack([k_mine, qk_from[:, 2 * HD :]])
    q1, q2, q3 = (rotate(q_pair, "x", d) for d in (1, 2, 3))

    pieces = tuple(rotate(half, "head", d) for d in (1, 2, 3))
    w_rows = rows_call(place, after(w_value[0], k_pair))
    *pieces, k_pair, q1, q3, w0, w1, w2, w3 = lax.optimization_barrier(pieces + (k_pair, q1, q3) + tuple(w_rows))
    halves = jnp.stack([half] + pieces)
    d_mine, d_theirs = dout(place, w_out[0], halves, rotate(halves, "layer", 1))
    d_pair = jnp.stack([d_mine, rotate(d_theirs, "z0", 1)])
    grads = [d_pair] + [rotate(d_pair, "x", d) for d in (1, 2, 3)]
    k_pair = after(k_pair, d_mine)
    k_all = [k_pair] + [rotate(k_pair, "z1", e) for e in (1, 2, 3)]
    w1, w3 = rotate(after(w1, d_mine), "head", 1), rotate(after(w3, d_mine), "head", 3)
    w2 = rotate(after(w2, w1, w3), "head", 2)

    none = jnp.zeros((NX, 4, BLK), jnp.float32)
    q_all = (q_pair, q1, q2, q3)
    expo0, sums = expo_call(0, place, none, q_all, k_all[0], k_all[1])
    expo2, sums = expo_call(2, place, sums, q_all, k_all[2], k_all[3])
    sums = after(sums, w1, w3)
    sums = [sums] + [rotate(sums, "x", d) for d in (1, 2, 3)]

    near, *far = grads_call(place, expo0, expo2, grads, sums)
    far = [along_pairs(far[e - 1], e, True) for e in (1, 2, 3)]
    mine, theirs = total_call(place, after(near, w2), far)
    v_pair = jnp.stack([mine, rotate(theirs, "z0", 1)])
    values = [v_pair] + [rotate(v_pair, "head", d) for d in (1, 2, 3)]
    contrib, sent = contrib_call(place, values, (w0, w1, w2, w3), gain, inv_rms.reshape(BLK, 1))
    higher = lax.ppermute(sent, "layer", [(1, 0)])
    resid, mine, *parts = edges_call(place, active[0], seed_grad, contrib, higher, decoder_pool[0])
    for d in (1, 2, 3):
        mine = mine + rotate(parts[d - 1], "head", d).astype(jnp.float32)
    edges = (mine * feature_acts[0].astype(jnp.float32)).astype(jnp.bfloat16)
    return edges[None], resid[None]


def solution(mesh):
    fine = Mesh(mesh.devices.reshape(2, NP, 2, NX, 4), ("layer", "z1", "z0", "x", "head"))
    seq = ("z1", "z0", "x")
    placed = (
        P(seq, "head"),
        P("layer", seq, "head"),
        P("layer", seq, "head"),
        P("layer", "head", None),
        P("layer", None, "head"),
        P("layer", None),
        P("layer", seq),
        P("layer", None, None, "head"),
        P("layer", seq, None),
        P("layer", seq, "head", None, None),
    )
    return jax.shard_map(
        local,
        mesh=fine,
        in_specs=placed,
        out_specs=(P("layer", seq, "head", None, None), P("layer", seq, "head")),
        check_vma=False,
    )
```

```python
import functools
import math

import jax
import jax.numpy as jnp
from jax import lax
from jax.experimental import pallas as pl
from jax.experimental.pallas import tpu as pltpu
from jax.sharding import Mesh, PartitionSpec as P

HD = 128
TILE = 128
WINDOW = 4096
SOFTCAP = 50.0
TO_TANH = 1.0 / 12.0 / SOFTCAP
TO_EXP2 = SOFTCAP * math.log2(math.e)

NX = 4
NP = 4
BLK = 256


def rotate(a, axis, d):
    n = lax.axis_size(axis)
    return lax.ppermute(a, axis, [(i, (i + d) % n) for i in range(n)])


def along_pairs(a, e, back):
    pairs = []
    for layer in range(2):
        for z1 in range(NP - e):
            near, far = layer * NP + z1, layer * NP + z1 + e
            if layer == 1 or e * 2 - 1 <= WINDOW // (BLK * NX):
                pairs.append((far, near) if back else (near, far))
    return lax.ppermute(a, ("layer", "z1"), pairs)


def after(a, *others):
    return lax.optimization_barrier((a,) + others)[0]


def nt_dot(a, b):
    return lax.dot_general(a, b, (((1,), (1,)), ((), ())), preferred_element_type=jnp.float32)


VM = pl.BlockSpec(memory_space=pltpu.VMEM)
SM = pl.BlockSpec(memory_space=pltpu.SMEM)
HB = pl.BlockSpec(memory_space=pltpu.HBM)


def in_hbm(a):
    return pltpu.with_memory_space_constraint(a, pltpu.HBM)


def params(mib, us):
    return dict(
        compiler_params=pltpu.CompilerParams(vmem_limit_bytes=mib * 1024 * 1024),
        cost_estimate=pl.CostEstimate(flops=int(us * 1e9), bytes_accessed=0, transcendentals=0),
    )


def parts_kernel(place, seed, q, k, gain, half, q_mine, k_mine, qk_theirs, gain_cols, sems):
    z0, layer, y = place[1], place[3], place[4]
    cols = half.shape[1]
    moves = (
        (seed.at[pl.ds(pl.multiple_of(layer * (BLK // 2), BLK // 2), BLK // 2), :], half),
        (q.at[:, pl.ds(pl.multiple_of((1 - z0) * 2 * HD, 2 * HD), 2 * HD)], qk_theirs.at[:, : 2 * HD]),
        (k.at[:, pl.ds(pl.multiple_of((1 - z0) * HD, HD), HD)], qk_theirs.at[:, 2 * HD :]),
        (q.at[:, pl.ds(pl.multiple_of(z0 * 2 * HD, 2 * HD), 2 * HD)], q_mine),
        (k.at[:, pl.ds(pl.multiple_of(z0 * HD, HD), HD)], k_mine),
        (gain.at[:, pl.ds(pl.multiple_of(y * cols, 128), cols)], gain_cols),
    )
    copies = [pltpu.make_async_copy(a, b, sems.at[i]) for i, (a, b) in enumerate(moves)]
    for copy in copies:
        copy.start()
    for copy in copies:
        copy.wait()


def parts_call(place, seed, q, k, gain):
    cols = seed.shape[1]
    b16 = jnp.bfloat16
    return pl.pallas_call(
        parts_kernel,
        out_shape=(
            jax.ShapeDtypeStruct((BLK // 2, cols), b16),
            jax.ShapeDtypeStruct((BLK, 2 * HD), b16),
            jax.ShapeDtypeStruct((BLK, HD), b16),
            jax.ShapeDtypeStruct((BLK, 3 * HD), b16),
            jax.ShapeDtypeStruct((1, cols), jnp.float32),
        ),
        in_specs=[SM] + [HB] * 4,
        out_specs=(VM,) * 5,
        scratch_shapes=[pltpu.SemaphoreType.DMA((6,))],
        name="parts",
        **params(8, 1),
    )(place, in_hbm(seed), in_hbm(q), in_hbm(k), in_hbm(gain))


def rows_kernel(place, w, *refs):
    outs, sems = refs[:4], refs[4]
    y = place[4]
    cols = outs[0].shape[0]
    copies = []
    for d, out in enumerate(outs):
        rows = pl.ds(pl.multiple_of(lax.rem(y + d, 4) * cols, 128), cols)
        copies.append(pltpu.make_async_copy(w.at[rows, :], out, sems.at[d]))
        copies[d].start()
    for copy in copies:
        copy.wait()


def rows_call(place, w):
    shape = jax.ShapeDtypeStruct((w.shape[0] // 4, w.shape[1]), w.dtype)
    return pl.pallas_call(
        rows_kernel,
        out_shape=(shape,) * 4,
        in_specs=[SM, HB],
        out_specs=(VM,) * 4,
        scratch_shapes=[pltpu.SemaphoreType.DMA((4,))],
        name="rows",
        **params(12, 1),
    )(place, in_hbm(w))


def total_kernel(place, near, far0, far1, far2, mine, theirs):
    for r, out in ((1, theirs), (0, mine)):
        total = near[r]
        for far in (far0, far1, far2):
            total += far[r].astype(jnp.float32)
        out[...] = total.astype(out.dtype)


def total_call(place, near, far):
    shape = jax.ShapeDtypeStruct((BLK, HD), jnp.bfloat16)
    return pl.pallas_call(
        total_kernel,
        out_shape=(shape, shape),
        in_specs=[SM] + [VM] * 4,
        out_specs=(VM, VM),
        name="total",
        **params(8, 1),
    )(place, near, *far)


def dout_kernel(place, w, own, other, mine, theirs):
    z0, layer, y = place[1], place[3], place[4]
    cols = own.shape[2]
    part = BLK // 2
    for out, half in ((theirs, 1 - z0), (mine, z0)):
        rows = pl.ds(pl.multiple_of(half * 2 * HD, 2 * HD), 2 * HD)
        total = jnp.zeros((BLK, 2 * HD), jnp.float32)
        for d in range(4):
            first = pl.multiple_of(lax.rem(y - d + 4, 4) * cols, 128)
            both = jnp.concatenate([own[d], other[d]], axis=0)
            total += nt_dot(both, w[rows, pl.ds(first, cols)])
        total = total.astype(jnp.bfloat16)
        out[pl.ds(pl.multiple_of(layer * part, part), part), :] = total[:part]
        out[pl.ds(pl.multiple_of((1 - layer) * part, part), part), :] = total[part:]


def dout(place, w, own, other):
    shape = jax.ShapeDtypeStruct((BLK, 2 * HD), jnp.bfloat16)
    return pl.pallas_call(
        dout_kernel,
        out_shape=(shape, shape),
        in_specs=[SM, VM, VM, VM],
        out_specs=(VM, VM),
        name="dout",
        **params(16, 3),
    )(place, w, own, other)


def weigh(s):
    return jnp.exp2(jnp.tanh(s * TO_TANH) * TO_EXP2)


def expo_kernel(first, place, before, queries, near, far, expo, sums, acc, ahead):
    z1, z0, x, layer = place[0], place[1], place[2], place[3]
    acc[...] = jnp.zeros_like(acc)
    ahead[...] = lax.broadcasted_iota(jnp.int32, (BLK, BLK), 1) - lax.broadcasted_iota(jnp.int32, (BLK, BLK), 0)
    x_at = [lax.rem(x - d + NX, NX) for d in range(NX)]
    for e, keys in ((first, near), (first + 1, far)):

        def step(key_r, carry, e=e, keys=keys):
            kb = 2 * (e - first) + key_r
            k = keys[key_r]

            def work(r, mask):
                for d in range(NX):
                    for g in range(2):
                        ex = weigh(nt_dot(k, queries[d][r, :, g * HD : (g + 1) * HD]))
                        if mask is not None:
                            ex = jnp.where(mask(x_at[d]), ex, 0.0)
                        acc[g, d, r] += jnp.sum(ex.reshape(BLK // 8, 8, BLK), axis=0)
                        col = pl.multiple_of((g * 8 + d * 2 + r) * BLK, BLK)
                        expo[kb, :, pl.ds(col, BLK)] = ex.astype(jnp.bfloat16)

            def full():
                def one(r, carry):
                    work(r, None)
                    return carry

                lax.fori_loop(0, 2, one, 0)

            def mixed():
                def one(r, carry):
                    apart = 2 * e + (z0 ^ r) - (z0 ^ key_r)
                    if e == 0:
                        all_kept, none_kept = apart > 0, apart < 0
                        mask = lambda at: ahead[...] >= (x - at) * BLK
                    else:
                        all_kept, none_kept = apart * BLK * NX < WINDOW, apart * BLK * NX > WINDOW
                        mask = lambda at: ahead[...] < (x - at) * BLK

                    @pl.when(all_kept)
                    def _():
                        work(r, None)

                    @pl.when(none_kept)
                    def _():
                        for d in range(NX):
                            for g in range(2):
                                col = pl.multiple_of((g * 8 + d * 2 + r) * BLK, BLK)
                                expo[kb, :, pl.ds(col, BLK)] = jnp.zeros((BLK, BLK), jnp.bfloat16)

                    @pl.when(jnp.logical_not(all_kept | none_kept))
                    def _():
                        work(r, mask)

                    return carry

                lax.fori_loop(0, 2, one, 0)

            if e == 0:
                mixed()
            elif e == 2:
                pl.when(layer == 1)(full)
                pl.when(layer == 0)(mixed)
            else:
                full()
            return carry

        @pl.when(reached(e, z1, layer))
        def _(step=step):
            lax.fori_loop(0, 2, step, 0)

    for d in range(NX):
        for r in range(2):
            for g in range(2):
                row = r * 2 + g
                total = jnp.sum(acc[g, d, r], axis=0, keepdims=True)
                sums[x_at[d], row : row + 1, :] = total + before[x_at[d], row : row + 1, :]


def reached(e, z1, layer):
    return (e <= z1) & ((layer == 1) | (e * 2 - 1 <= WINDOW // (BLK * NX)))


def expo_call(first, place, before, queries, near, far):
    def kernel(place, before, q0, q1, q2, q3, *refs):
        expo_kernel(first, place, before, (q0, q1, q2, q3), *refs)

    return pl.pallas_call(
        kernel,
        out_shape=(
            pltpu.VMEM((4, BLK, 16 * BLK), jnp.bfloat16),
            jax.ShapeDtypeStruct((NX, 4, BLK), jnp.float32),
        ),
        in_specs=[SM] + [VM] * 7,
        out_specs=(VM, VM),
        scratch_shapes=[pltpu.VMEM((2, NX, 2, 8, BLK), jnp.float32), pltpu.VMEM((BLK, BLK), jnp.int32)],
        name=f"expo{first}",
        **params(10, 4),
    )(place, before, *queries, near, far)


def grads_kernel(place, expo0, expo2, *refs):
    grads, sums, outs, scaled = refs[0:4], refs[4:8], refs[8:12], refs[12]
    z1, x, layer = place[0], place[2], place[3]
    for d in range(NX):
        at = lax.rem(x - d + NX, NX)
        inverse = 1.0 / (sums[0][at] + sums[1][at] + sums[2][at] + sums[3][at])
        inverse = jnp.concatenate([inverse, inverse], axis=0).T
        for r in range(2):
            for g in range(2):
                piece = grads[d][r, :, g * HD : (g + 1) * HD].astype(jnp.float32)
                row = r * 2 + g
                col = (g * 8 + d * 2 + r) * BLK
                scaled[col : col + BLK] = (piece * inverse[:, row : row + 1]).astype(jnp.bfloat16)
    for e in range(4):
        used = reached(e, z1, layer)
        expo = (expo0, expo2)[e // 2]

        @pl.when(used)
        def _(e=e, expo=expo):
            for r in range(2):
                dots = jnp.dot(expo[e % 2 * 2 + r], scaled[...], preferred_element_type=jnp.float32)
                outs[e][r] = dots.astype(outs[e].dtype)

        @pl.when(jnp.logical_not(used))
        def _(e=e):
            outs[e][...] = jnp.zeros_like(outs[e])


def grads_call(place, expo0, expo2, grads, sums):
    far = jax.ShapeDtypeStruct((2, BLK, HD), jnp.bfloat16)
    return pl.pallas_call(
        grads_kernel,
        out_shape=(jax.ShapeDtypeStruct((2, BLK, HD), jnp.float32), far, far, far),
        in_specs=[SM] + [VM] * 10,
        out_specs=(VM,) * 4,
        scratch_shapes=[pltpu.VMEM((16 * BLK, HD), jnp.bfloat16)],
        name="value_grads",
        **params(12, 7),
    )(
        place,
        pltpu.with_memory_space_constraint(expo0, pltpu.VMEM),
        pltpu.with_memory_space_constraint(expo2, pltpu.VMEM),
        *grads,
        *sums,
    )


def contrib_of(place, refs):
    values, weights, gain, inv = refs[0:4], refs[4:8], refs[8], refs[9]
    z0 = place[1]
    total = jnp.zeros((BLK, gain.shape[1]), jnp.float32)
    for v, w in zip(values, weights):
        total += nt_dot(jnp.concatenate([v[z0], v[1 - z0]], axis=1), w[...])
    return total * gain[...] * inv[...]


def upper_kernel(place, *refs):
    out, sent = refs[10:]

    @pl.when(place[3] == 1)
    def _():
        total = contrib_of(place, refs)
        out[...] = total
        sent[...] = total.astype(sent.dtype)

    @pl.when(place[3] == 0)
    def _():
        sent[...] = jnp.zeros_like(sent)


def lower_kernel(place, *refs):
    upper, out = refs[10:]

    @pl.when(place[3] == 0)
    def _():
        out[...] = contrib_of(place, refs)

    @pl.when(place[3] == 1)
    def _():
        out[...] = upper[...]


def upper_call(place, values, weights, gain, inv):
    shape = (BLK, gain.shape[1])
    return pl.pallas_call(
        upper_kernel,
        out_shape=(jax.ShapeDtypeStruct(shape, jnp.float32), jax.ShapeDtypeStruct(shape, jnp.bfloat16)),
        in_specs=[SM] + [VM] * 10,
        out_specs=(VM, VM),
        name="upper",
        **params(12, 1),
    )(place, *values, *weights, gain, inv)


def lower_call(place, values, weights, gain, inv, upper):
    return pl.pallas_call(
        lower_kernel,
        out_shape=jax.ShapeDtypeStruct(upper.shape, jnp.float32),
        in_specs=[SM] + [VM] * 11,
        out_specs=VM,
        name="lower",
        **params(12, 2),
    )(place, *values, *weights, gain, inv, upper)


def edges_kernel(place, active, seed, contrib, higher, pool, resid, own, *far):
    y = place[4]
    resid[...] = (seed[...].astype(jnp.float32) + (higher[...].astype(jnp.float32) + contrib[...])).astype(jnp.bfloat16)
    for d in range(4):
        owner = lax.rem(y + d, 4)
        for t in range(2):
            rows = resid[t * TILE : (t + 1) * TILE, :]
            for k in range(2):
                slot = active[t, owner * 2 + k]
                dots = nt_dot(rows, pool[jnp.maximum(slot, 0)])
                dots = jnp.where(slot >= 0, dots, 0.0)
                if d == 0:
                    own[t, k] = dots
                else:
                    far[d - 1][t, k] = dots.astype(jnp.bfloat16)


def edges_call(place, active, seed, contrib, higher, pool):
    far = jax.ShapeDtypeStruct((2, 2, TILE, TILE), jnp.bfloat16)
    return pl.pallas_call(
        edges_kernel,
        out_shape=(
            jax.ShapeDtypeStruct(seed.shape, jnp.bfloat16),
            jax.ShapeDtypeStruct((2, 2, TILE, TILE), jnp.float32),
            far,
            far,
            far,
        ),
        in_specs=[SM, SM] + [VM] * 4,
        out_specs=(VM,) * 5,
        name="edges",
        **params(12, 3),
    )(place, active, seed, contrib, higher, pool)


def local(
    seed_grad,
    queries,
    key_cache,
    w_out,
    w_value,
    norm_gain,
    inv_rms,
    decoder_pool,
    active,
    feature_acts,
):
    z1, z0, x, y, layer = (lax.axis_index(a) for a in ("z1", "z0", "x", "head", "layer"))
    place = jnp.stack([z1, z0, x, layer, y]).astype(jnp.int32)
    cols = seed_grad.shape[1]
    half, q_mine, k_mine, qk_theirs, gain = parts_call(place, seed_grad, queries[0], key_cache[0], norm_gain)

    qk_from = rotate(qk_theirs, "z0", 1)
    q_pair = jnp.stack([q_mine, qk_from[:, : 2 * HD]])
    k_pair = jnp.stack([k_mine, qk_from[:, 2 * HD :]])
    q1, q2, q3 = (rotate(q_pair, "x", d) for d in (1, 2, 3))

    pieces = tuple(rotate(half, "head", d) for d in (1, 2, 3))
    w_rows = rows_call(place, after(w_value[0], k_pair))
    *pieces, k_pair, q1, q3, w0, w1, w2, w3 = lax.optimization_barrier(pieces + (k_pair, q1, q3) + tuple(w_rows))
    halves = jnp.stack([half] + pieces)
    d_mine, d_theirs = dout(place, w_out[0], halves, rotate(halves, "layer", 1))
    d_pair = jnp.stack([d_mine, rotate(d_theirs, "z0", 1)])
    grads = [d_pair] + [rotate(d_pair, "x", d) for d in (1, 2, 3)]
    k_pair = after(k_pair, d_mine)
    k_all = [k_pair] + [rotate(k_pair, "z1", e) for e in (1, 2, 3)]
    w1, w3 = rotate(after(w1, d_mine), "head", 1), rotate(after(w3, d_mine), "head", 3)
    w2 = rotate(after(w2, w1, w3), "head", 2)

    none = jnp.zeros((NX, 4, BLK), jnp.float32)
    q_all = (q_pair, q1, q2, q3)
    expo0, sums = expo_call(0, place, none, q_all, k_all[0], k_all[1])
    expo2, sums = expo_call(2, place, sums, q_all, k_all[2], k_all[3])
    sums = after(sums, w1, w3)
    sums = [sums] + [rotate(sums, "x", d) for d in (1, 2, 3)]

    near, *far = grads_call(place, expo0, expo2, grads, sums)
    far = [along_pairs(far[e - 1], e, True) for e in (1, 2, 3)]
    mine, theirs = total_call(place, after(near, w2), far)
    v_pair = jnp.stack([mine, rotate(theirs, "z0", 1)])
    values = [v_pair] + [rotate(v_pair, "head", d) for d in (1, 2, 3)]
    given = (place, values, (w0, w1, w2, w3), gain, inv_rms.reshape(BLK, 1))
    upper, sent = upper_call(*given)
    higher = lax.ppermute(sent, "layer", [(1, 0)])
    contrib = lower_call(*given, upper)
    resid, mine, *parts = edges_call(place, active[0], seed_grad, contrib, higher, decoder_pool[0])
    for d in (1, 2, 3):
        mine = mine + rotate(parts[d - 1], "head", d).astype(jnp.float32)
    edges = (mine * feature_acts[0].astype(jnp.float32)).astype(jnp.bfloat16)
    return edges[None], resid[None]


def solution(mesh):
    fine = Mesh(mesh.devices.reshape(2, NP, 2, NX, 4), ("layer", "z1", "z0", "x", "head"))
    seq = ("z1", "z0", "x")
    placed = (
        P(seq, "head"),
        P("layer", seq, "head"),
        P("layer", seq, "head"),
        P("layer", "head", None),
        P("layer", None, "head"),
        P("layer", None),
        P("layer", seq),
        P("layer", None, None, "head"),
        P("layer", seq, None),
        P("layer", seq, "head", None, None),
    )
    return jax.shard_map(
        local,
        mesh=fine,
        in_specs=placed,
        out_specs=(P("layer", seq, "head", None, None), P("layer", seq, "head")),
        check_vma=False,
    )
```
